32 devices in a mesh: pipe: 2 (over core), dp: 16 (over z, y, x).
Axes of the slice: x: 2, y: 2, z: 4, core: 2. Of those that a mesh axis runs over, the one named last changes fastest.
Arguments:
- gate: bfloat16 [2, 1, 2048, 4096], P('pipe', None, 'dp'), may hold values from -5 to 5
- filters: bfloat16 [2, 256, 128], P('pipe', 'dp'), may hold values from -0.75 to 0.75
- doc_ids: int32 [1, 2048], P(None, 'dp'), may hold values from 0 to 1, as said below
- loss_grad: bfloat16 [1, 2048, 4096], P(None, 'dp'), may hold values from -6 to 6
Outputs:
- input_grads: bfloat16 [2, 1, 2048, 4096], P('pipe', None, 'dp')
The draws below stay inside these ranges and needn't reach their ends.
Inputs may be any that keep to these rules, and one draw needn't show every extreme that they name: `doc_ids`: within each window the ids never fall, begin at 0 and end at 1, and every document holds 128 or more tokens.
All inputs are finite; a program needn't handle non-finite values.
Results may differ from the reference program's by a relative error of at most 0.0049.
Values may be sent and summed in bfloat16 or wider, within the bound.
A program may use at most 64 MiB of HBM per device.

```python
import jax
import jax.numpy as jnp
from jax import lax

C = 4096
GROUPS = 256
FILTER = 128
M = 1
TOKENS_MB = 2048
LAYERS = 2
DOCS = 2


def draw_doc_ids(key, part):
    spare_tokens = TOKENS_MB - DOCS * FILTER
    cut_points = jax.random.randint(key, (M, DOCS - 1), 0, spare_tokens + 1)
    cut_points = jnp.sort(cut_points, axis=1)
    starts = cut_points + FILTER * jnp.arange(1, DOCS, dtype=jnp.int32)[None, :]
    position = jnp.arange(TOKENS_MB, dtype=jnp.int32)
    return jnp.sum((position[None, :, None] >= starts[:, None, :]).astype(jnp.int32), axis=2).astype(jnp.int32)


def shard_levels(key, extent, cuts, smallest, largest):
    gain, own = 1.0, jax.random.fold_in(key, 6)
    for dim, parts in cuts:
        draws = jnp.exp(jax.random.uniform(jax.random.fold_in(own, dim), (parts,), jnp.float32, smallest / len(cuts), largest / len(cuts)))
        gain = gain * jnp.repeat(draws, extent[dim] // parts).reshape([-1 if axis == dim else 1 for axis in range(len(extent))])
    return gain


def normal_values(own_key, extent, width, bound, cuts=(), kind=jnp.bfloat16):
    values = jax.random.normal(own_key, extent, jnp.float32) * width
    if len(cuts) > 0:
        values = shard_levels(own_key, extent, cuts, -0.22, 0.18) * values
    return jnp.clip(values, min=-bound, max=bound).astype(kind)


def setup_inputs(seed: int = 0) -> dict:
    keys = jax.random.split(jax.random.key(seed), 5)
    gate = normal_values(keys[0], (LAYERS, M, TOKENS_MB, C), 1.0, 5.0, ((0, 2), (2, 16)))
    filters = normal_values(keys[1], (LAYERS, GROUPS, FILTER), (0.6 / FILTER ** 0.5), 0.75, ((0, 2), (1, 16)))
    doc_ids = draw_doc_ids(jax.random.fold_in(keys[4], 71), 0)
    loss_grad = normal_values(keys[3], (M, TOKENS_MB, C), 1.0, 6.0, ((1, 16),))
    return {"gate": gate, "filters": filters, "doc_ids": doc_ids, "loss_grad": loss_grad}


def adjoint_all(scaled, parity, filt_all):
    micro_count, length, channels = scaled.shape
    groups, tap_count = filt_all.shape
    padded_len = 2 * length
    kernel = jnp.repeat(filt_all.astype(jnp.float32), channels // groups, axis=0)
    kernel_hat = jnp.conj(jnp.fft.rfft(kernel, n=padded_len, axis=1)).T
    summed = jnp.zeros((micro_count, length, channels), jnp.float32)
    for colour in (0, 1):
        chosen = (parity == colour)[..., None]
        masked = jnp.where(chosen, scaled.astype(jnp.float32), jnp.float32(0.0))
        spectrum = jnp.fft.rfft(masked, n=padded_len, axis=1)
        correlated = jnp.fft.irfft(spectrum * kernel_hat[None], n=padded_len, axis=1)[:, :length]
        summed = summed + jnp.where(chosen, correlated, jnp.float32(0.0))
    return summed


def reference(gate, filters, doc_ids, loss_grad):
    parity = (doc_ids % 2).astype(jnp.int32)

    def one_layer(incoming, inputs):
        gate_layer, filt_all = inputs
        scaled = (gate_layer.astype(jnp.float32) * incoming.astype(jnp.float32)).astype(jnp.bfloat16)
        update = adjoint_all(scaled, parity, filt_all)
        result = (incoming.astype(jnp.float32) + update).astype(jnp.bfloat16)
        return result, result

    _, outputs = lax.scan(one_layer, loss_grad, (gate, filters), reverse=True)
    return outputs
```

```python
import functools

import jax
import jax.numpy as jnp
from jax import lax
from jax.experimental import pallas as pl
from jax.experimental.pallas import tpu as pltpu
from jax.sharding import PartitionSpec as P

MESH_ID = pl.DeviceIdType.MESH
CHUNK = 256
LAG = 2


def kernel(
    dp_count, pipe_count, lane_width, slot_groups,
    gate, filt, docs, loss, out,
    gbuf, inc, sbuf, halo, obuf, fall, table, docs_own, docs_next, mask_own, mask_next,
    gsem, lsem, osem, fsend, frecv, hsend, hrecv, psend, precv, dsend, drecv,
):
    chunk_count, rows, width = sbuf.shape
    groups = width // lane_width
    slots = groups // slot_groups
    stage = lax.axis_index("pipe")
    me = lax.axis_index("dp")
    is_last_stage = stage == pipe_count - 1
    not_last_stage = stage < pipe_count - 1
    has_below = stage > 0
    has_before = me > 0
    has_next = me < dp_count - 1

    def columns(j):
        return pl.ds(pl.multiple_of(j * width, width), width)

    def gate_copy(j):
        return pltpu.make_async_copy(gate.at[0, 0, :, columns(j)], gbuf.at[j], gsem.at[j])

    def loss_copy(j):
        return pltpu.make_async_copy(loss.at[0, :, columns(j)], inc.at[j], lsem.at[j])

    def out_copy(j):
        return pltpu.make_async_copy(obuf.at[j], out.at[0, 0, :, columns(j)], osem.at[j])

    def filter_copy(slot, peer):
        return pltpu.make_async_remote_copy(
            src_ref=filt, dst_ref=fall.at[slot], send_sem=fsend.at[peer], recv_sem=frecv.at[slot],
            device_id=(stage, peer), device_id_type=MESH_ID,
        )

    def halo_copy(j):
        return pltpu.make_async_remote_copy(
            src_ref=sbuf.at[j], dst_ref=halo.at[j], send_sem=hsend.at[j], recv_sem=hrecv.at[j],
            device_id=(stage, me - 1), device_id_type=MESH_ID,
        )

    def docs_copy():
        return pltpu.make_async_remote_copy(
            src_ref=docs_own, dst_ref=docs_next, send_sem=dsend, recv_sem=drecv,
            device_id=(stage, me - 1), device_id_type=MESH_ID,
        )

    def pipe_copy(j):
        return pltpu.make_async_remote_copy(
            src_ref=obuf.at[j], dst_ref=inc.at[j], send_sem=psend.at[j], recv_sem=precv.at[j],
            device_id=(stage - 1, me), device_id_type=MESH_ID,
        )

    def each(count, fn):
        def step(j, carry):
            fn(j)
            return carry
        lax.fori_loop(0, count, step, 0)

    each(chunk_count, lambda j: gate_copy(j).start())

    @pl.when(is_last_stage)
    def _():
        each(chunk_count, lambda j: loss_copy(j).start())

    barrier = pltpu.get_barrier_semaphore()

    def greet(k):
        pl.semaphore_signal(
            barrier, inc=1, device_id=(stage, lax.rem(me + k + 1, dp_count)), device_id_type=MESH_ID
        )

    each(dp_count - 1, greet)

    @pl.when(has_below)
    def _():
        pl.semaphore_signal(barrier, inc=1, device_id=(stage - 1, me), device_id_type=MESH_ID)

    @pl.when(not_last_stage)
    def _():
        pl.semaphore_signal(barrier, inc=1, device_id=(stage + 1, me), device_id_type=MESH_ID)

    docs_own[...] = jnp.broadcast_to(docs[...], docs_own.shape)
    fall[me] = filt[...]

    greeted = dp_count - 1 + has_below.astype(jnp.int32) + not_last_stage.astype(jnp.int32)
    pl.semaphore_wait(barrier, greeted)

    def send_filters(k):
        peer = lax.rem(me + k + 1, dp_count)
        filter_copy(me, peer).start()

    @pl.when(has_before)
    def _():
        docs_copy().start()

    each(dp_count - 1, send_filters)

    def scale(j):
        gate_copy(j).wait()

        @pl.when(is_last_stage)
        def _():
            loss_copy(j).wait()

        @pl.when(not_last_stage)
        def _():
            pltpu.make_async_remote_copy(
                src_ref=obuf.at[j], dst_ref=inc.at[j], send_sem=psend.at[j], recv_sem=precv.at[j],
                device_id=(stage + 1, me), device_id_type=MESH_ID,
            ).wait_recv()

        sbuf[j] = (gbuf[j].astype(jnp.float32) * inc[j].astype(jnp.float32)).astype(jnp.bfloat16)

        @pl.when(has_before)
        def _():
            halo_copy(j).start()

    @pl.when(is_last_stage)
    def _():
        each(chunk_count, scale)

    @pl.when(jnp.logical_not(has_next))
    def _():
        docs_next[...] = jnp.zeros_like(docs_next)

        def clear(j):
            halo[j] = jnp.zeros((rows, width), jnp.bfloat16)

        each(chunk_count, clear)

    @pl.when(has_next)
    def _():
        pltpu.make_async_remote_copy(
            src_ref=docs_own, dst_ref=docs_next, send_sem=dsend, recv_sem=drecv,
            device_id=(stage, me + 1), device_id_type=MESH_ID,
        ).wait_recv()

    at_row = lax.broadcasted_iota(jnp.int32, (rows, rows), 0)
    at_col = lax.broadcasted_iota(jnp.int32, (rows, rows), 1)
    own_cols = jnp.broadcast_to(docs_own[0:1, :], (rows, rows)).astype(jnp.float32)
    next_cols = jnp.broadcast_to(docs_next[0:1, :], (rows, rows)).astype(jnp.float32)
    own_rows = own_cols.T
    one, zero = jnp.float32(1.0), jnp.float32(0.0)
    mask_own[...] = jnp.where(
        jnp.logical_and(at_col >= at_row, own_rows == own_cols), one, zero
    ).astype(jnp.bfloat16)
    mask_next[...] = jnp.where(
        jnp.logical_and(at_col < at_row, own_rows == next_cols), one, zero
    ).astype(jnp.bfloat16)

    def make_table(j):
        for q in range(slots):
            slot = j * slots + q

            @pl.when(slot != me)
            def _():
                filter_copy(slot, slot).wait_recv()

        for q in range(slots):
            taps = fall[j * slots + q].astype(jnp.float32)
            for r in range(slot_groups):
                g = q * slot_groups + r
                spread = jnp.broadcast_to(taps[r : r + 1, :], (rows, rows))
                turned = pltpu.roll(spread, 0, 1, stride=1, stride_axis=0).astype(jnp.bfloat16)
                table[g * rows : (g + 1) * rows, :rows] = turned * mask_own[...]
                table[g * rows : (g + 1) * rows, rows:] = turned * mask_next[...]

    def produce(j):
        @pl.when(has_next)
        def _():
            pltpu.make_async_remote_copy(
                src_ref=sbuf.at[j], dst_ref=halo.at[j], send_sem=hsend.at[j], recv_sem=hrecv.at[j],
                device_id=(stage, me + 1), device_id_type=MESH_ID,
            ).wait_recv()

        slab = jnp.concatenate([sbuf[j], halo[j]], axis=0)
        group_of = lax.broadcasted_iota(jnp.int32, (rows, width), 1) // lane_width
        total = inc[j].astype(jnp.float32)
        update = jnp.zeros((rows, width), jnp.float32)
        for g in range(groups):
            part = jnp.dot(
                table[g * rows : (g + 1) * rows, :], slab, preferred_element_type=jnp.float32
            )
            update = jnp.where(group_of == g, part, update)
        obuf[j] = (total + update).astype(jnp.bfloat16)

        @pl.when(has_below)
        def _():
            pipe_copy(j).start()

        out_copy(j).start()

    def step(s):
        @pl.when(s >= LAG)
        def _():
            make_table(s - LAG)

        @pl.when(jnp.logical_and(not_last_stage, s < chunk_count))
        def _():
            scale(s)

        @pl.when(s >= LAG)
        def _():
            produce(s - LAG)

    each(chunk_count + LAG, step)

    def finish(j):
        out_copy(j).wait()

        @pl.when(has_below)
        def _():
            pipe_copy(j).wait_send()

        @pl.when(has_before)
        def _():
            halo_copy(j).wait_send()

    each(chunk_count, finish)

    @pl.when(has_before)
    def _():
        docs_copy().wait_send()

    each(dp_count - 1, lambda k: filter_copy(me, lax.rem(me + k + 1, dp_count)).wait_send())


def body(mesh_shape, gate, filters, doc_ids, loss_grad):
    dp_count, pipe_count = mesh_shape["dp"], mesh_shape["pipe"]
    _, _, rows, channels = gate.shape
    slot_groups, taps = filters.shape[1:]
    lane_width = channels // (slot_groups * dp_count)
    chunk_count = channels // CHUNK
    slot_rows = -(-slot_groups // 16) * 16
    filt = filters[0]
    if slot_rows != slot_groups:
        filt = jnp.pad(filt, ((0, slot_rows - slot_groups), (0, 0)))
    chunks = pltpu.VMEM((chunk_count, rows, CHUNK), jnp.bfloat16)
    groups = CHUNK // lane_width
    dma = pltpu.SemaphoreType.DMA
    return pl.pallas_call(
        functools.partial(kernel, dp_count, pipe_count, lane_width, slot_groups),
        out_shape=jax.ShapeDtypeStruct(gate.shape, jnp.bfloat16),
        in_specs=[
            pl.BlockSpec(memory_space=pl.ANY),
            pl.BlockSpec(memory_space=pltpu.VMEM),
            pl.BlockSpec(memory_space=pltpu.VMEM),
            pl.BlockSpec(memory_space=pl.ANY),
        ],
        out_specs=pl.BlockSpec(memory_space=pl.ANY),
        scratch_shapes=[
            chunks, chunks, chunks, chunks, chunks,
            pltpu.VMEM((dp_count, slot_rows, taps), jnp.bfloat16),
            pltpu.VMEM((groups * rows, 2 * rows), jnp.bfloat16),
            pltpu.VMEM((8, rows), jnp.int32),
            pltpu.VMEM((8, rows), jnp.int32),
            pltpu.VMEM((rows, rows), jnp.bfloat16),
            pltpu.VMEM((rows, rows), jnp.bfloat16),
            dma((chunk_count,)), dma((chunk_count,)), dma((chunk_count,)),
            dma((dp_count,)), dma((dp_count,)),
            dma((chunk_count,)), dma((chunk_count,)),
            dma((chunk_count,)), dma((chunk_count,)),
            dma, dma,
        ],
        compiler_params=pltpu.CompilerParams(
            collective_id=0, has_side_effects=True, vmem_limit_bytes=40 * 1024 * 1024
        ),
        cost_estimate=pl.CostEstimate(
            flops=2 * 2 * rows * rows * channels * 16, bytes_accessed=6 * rows * channels, transcendentals=0
        ),
    )(gate, filt, doc_ids, loss_grad)


def solution(mesh):
    return jax.shard_map(
        functools.partial(body, dict(mesh.shape)),
        mesh=mesh,
        in_specs=(
            P("pipe", None, "dp", None),
            P("pipe", "dp", None),
            P(None, "dp"),
            P(None, "dp", None),
        ),
        out_specs=P("pipe", None, "dp", None),
        check_vma=False,
    )
```

```python
import functools

import jax
import jax.numpy as jnp
from jax import lax
from jax.experimental import pallas as pl
from jax.experimental.pallas import tpu as pltpu
from jax.sharding import PartitionSpec as P

MESH_ID = pl.DeviceIdType.MESH
CHUNK = 256
LAG = 5


def kernel(
    dp_count, pipe_count, lane_width, slot_groups,
    gate, filt_hbm, docs_hbm, loss, out,
    filt, docs, filt_sem, docs_sem, gbuf, inc, sbuf, halo, obuf, fall, table, docs_own, docs_next, mask_own, mask_next,
    gsem, lsem, osem, fsend, frecv, hsend, hrecv, psend, precv, dsend, drecv,
):
    chunk_count, rows, width = sbuf.shape
    groups = width // lane_width
    slots = groups // slot_groups
    stage = lax.axis_index("pipe")
    me = lax.axis_index("dp")
    is_last_stage = stage == pipe_count - 1
    not_last_stage = stage < pipe_count - 1
    has_below = stage > 0
    has_before = me > 0
    has_next = me < dp_count - 1

    def columns(j):
        return pl.ds(pl.multiple_of(j * width, width), width)

    def gate_copy(j):
        return pltpu.make_async_copy(gate.at[0, 0, :, columns(j)], gbuf.at[j], gsem.at[j])

    def loss_copy(j):
        return pltpu.make_async_copy(loss.at[0, :, columns(j)], inc.at[j], lsem.at[j])

    def out_copy(j):
        return pltpu.make_async_copy(obuf.at[j], out.at[0, 0, :, columns(j)], osem.at[j])

    def filter_copy(slot, peer):
        return pltpu.make_async_remote_copy(
            src_ref=filt, dst_ref=fall.at[slot], send_sem=fsend.at[peer], recv_sem=frecv.at[slot],
            device_id=(stage, peer), device_id_type=MESH_ID,
        )

    def halo_copy(j):
        return pltpu.make_async_remote_copy(
            src_ref=sbuf.at[j], dst_ref=halo.at[j], send_sem=hsend.at[j], recv_sem=hrecv.at[j],
            device_id=(stage, me - 1), device_id_type=MESH_ID,
        )

    def docs_copy():
        return pltpu.make_async_remote_copy(
            src_ref=docs_own, dst_ref=docs_next, send_sem=dsend, recv_sem=drecv,
            device_id=(stage, me - 1), device_id_type=MESH_ID,
        )

    def pipe_copy(j):
        return pltpu.make_async_remote_copy(
            src_ref=obuf.at[j], dst_ref=inc.at[j], send_sem=psend.at[j], recv_sem=precv.at[j],
            device_id=(stage - 1, me), device_id_type=MESH_ID,
        )

    def each(count, fn):
        def step(j, carry):
            fn(j)
            return carry
        lax.fori_loop(0, count, step, 0)

    load_filters = pltpu.make_async_copy(filt_hbm, filt, filt_sem)
    load_docs = pltpu.make_async_copy(docs_hbm, docs, docs_sem)
    load_filters.start()
    load_docs.start()
    each(chunk_count, lambda j: gate_copy(j).start())

    @pl.when(is_last_stage)
    def _():
        each(chunk_count, lambda j: loss_copy(j).start())

    barrier = pltpu.get_barrier_semaphore()

    def greet(k):
        pl.semaphore_signal(
            barrier, inc=1, device_id=(stage, lax.rem(me + k + 1, dp_count)), device_id_type=MESH_ID
        )

    each(dp_count - 1, greet)

    @pl.when(has_below)
    def _():
        pl.semaphore_signal(barrier, inc=1, device_id=(stage - 1, me), device_id_type=MESH_ID)

    @pl.when(not_last_stage)
    def _():
        pl.semaphore_signal(barrier, inc=1, device_id=(stage + 1, me), device_id_type=MESH_ID)

    load_filters.wait()
    load_docs.wait()
    docs_own[...] = jnp.broadcast_to(docs[...], docs_own.shape)
    fall[me] = filt[...]

    greeted = dp_count - 1 + has_below.astype(jnp.int32) + not_last_stage.astype(jnp.int32)
    pl.semaphore_wait(barrier, greeted)

    def send_filters(k):
        peer = lax.rem(me + k + 1, dp_count)
        filter_copy(me, peer).start()

    @pl.when(has_before)
    def _():
        docs_copy().start()

    each(dp_count - 1, send_filters)

    def scale(j):
        gate_copy(j).wait()

        @pl.when(is_last_stage)
        def _():
            loss_copy(j).wait()

        @pl.when(not_last_stage)
        def _():
            pltpu.make_async_remote_copy(
                src_ref=obuf.at[j], dst_ref=inc.at[j], send_sem=psend.at[j], recv_sem=precv.at[j],
                device_id=(stage + 1, me), device_id_type=MESH_ID,
            ).wait_recv()

        sbuf[j] = (gbuf[j].astype(jnp.float32) * inc[j].astype(jnp.float32)).astype(jnp.bfloat16)

        @pl.when(has_before)
        def _():
            halo_copy(j).start()

    @pl.when(is_last_stage)
    def _():
        each(chunk_count, scale)

    @pl.when(jnp.logical_not(has_next))
    def _():
        docs_next[...] = jnp.zeros_like(docs_next)

        def clear(j):
            halo[j] = jnp.zeros((rows, width), jnp.bfloat16)

        each(chunk_count, clear)

    @pl.when(has_next)
    def _():
        pltpu.make_async_remote_copy(
            src_ref=docs_own, dst_ref=docs_next, send_sem=dsend, recv_sem=drecv,
            device_id=(stage, me + 1), device_id_type=MESH_ID,
        ).wait_recv()

    at_row = lax.broadcasted_iota(jnp.int32, (rows, rows), 0)
    at_col = lax.broadcasted_iota(jnp.int32, (rows, rows), 1)
    own_cols = jnp.broadcast_to(docs_own[0:1, :], (rows, rows)).astype(jnp.float32)
    next_cols = jnp.broadcast_to(docs_next[0:1, :], (rows, rows)).astype(jnp.float32)
    own_rows = own_cols.T
    one, zero = jnp.float32(1.0), jnp.float32(0.0)
    mask_own[...] = jnp.where(
        jnp.logical_and(at_col >= at_row, own_rows == own_cols), one, zero
    ).astype(jnp.bfloat16)
    mask_next[...] = jnp.where(
        jnp.logical_and(at_col < at_row, own_rows == next_cols), one, zero
    ).astype(jnp.bfloat16)

    def make_table(j):
        for q in range(slots):
            slot = j * slots + q

            @pl.when(slot != me)
            def _():
                filter_copy(slot, slot).wait_recv()

        for q in range(slots):
            taps = fall[j * slots + q].astype(jnp.float32)
            for r in range(slot_groups):
                g = q * slot_groups + r
                spread = jnp.broadcast_to(taps[r : r + 1, :], (rows, rows))
                turned = pltpu.roll(spread, 0, 1, stride=1, stride_axis=0).astype(jnp.bfloat16)
                table[g * rows : (g + 1) * rows, :rows] = turned * mask_own[...]
                table[g * rows : (g + 1) * rows, rows:] = turned * mask_next[...]

    def produce(j):
        @pl.when(has_next)
        def _():
            pltpu.make_async_remote_copy(
                src_ref=sbuf.at[j], dst_ref=halo.at[j], send_sem=hsend.at[j], recv_sem=hrecv.at[j],
                device_id=(stage, me + 1), device_id_type=MESH_ID,
            ).wait_recv()

        slab = jnp.concatenate([sbuf[j], halo[j]], axis=0)
        group_of = lax.broadcasted_iota(jnp.int32, (rows, width), 1) // lane_width
        total = inc[j].astype(jnp.float32)
        update = jnp.zeros((rows, width), jnp.float32)
        parts = jnp.dot(table[...], slab, preferred_element_type=jnp.float32)
        for g in range(groups):
            update = jnp.where(group_of == g, parts[g * rows : (g + 1) * rows, :], update)
        obuf[j] = (total + update).astype(jnp.bfloat16)

        @pl.when(has_below)
        def _():
            pipe_copy(j).start()

        out_copy(j).start()

    def step(s):
        @pl.when(s >= LAG)
        def _():
            make_table(s - LAG)

        @pl.when(jnp.logical_and(not_last_stage, s < chunk_count))
        def _():
            scale(s)

        @pl.when(s >= LAG)
        def _():
            produce(s - LAG)

    each(chunk_count + LAG, step)

    def finish(j):
        out_copy(j).wait()

        @pl.when(has_below)
        def _():
            pipe_copy(j).wait_send()

        @pl.when(has_before)
        def _():
            halo_copy(j).wait_send()

    each(chunk_count, finish)

    @pl.when(has_before)
    def _():
        docs_copy().wait_send()

    each(dp_count - 1, lambda k: filter_copy(me, lax.rem(me + k + 1, dp_count)).wait_send())


def body(mesh_shape, gate, filters, doc_ids, loss_grad):
    dp_count, pipe_count = mesh_shape["dp"], mesh_shape["pipe"]
    _, _, rows, channels = gate.shape
    slot_groups, taps = filters.shape[1:]
    lane_width = channels // (slot_groups * dp_count)
    chunk_count = channels // CHUNK
    slot_rows = -(-slot_groups // 16) * 16
    filt = filters[0]
    if slot_rows != slot_groups:
        filt = jnp.pad(filt, ((0, slot_rows - slot_groups), (0, 0)))
    chunks = pltpu.VMEM((chunk_count, rows, CHUNK), jnp.bfloat16)
    groups = CHUNK // lane_width
    dma = pltpu.SemaphoreType.DMA
    return pl.pallas_call(
        functools.partial(kernel, dp_count, pipe_count, lane_width, slot_groups),
        out_shape=jax.ShapeDtypeStruct(gate.shape, jnp.bfloat16),
        in_specs=[
            pl.BlockSpec(memory_space=pl.ANY),
            pl.BlockSpec(memory_space=pl.ANY),
            pl.BlockSpec(memory_space=pl.ANY),
            pl.BlockSpec(memory_space=pl.ANY),
        ],
        out_specs=pl.BlockSpec(memory_space=pl.ANY),
        scratch_shapes=[
            pltpu.VMEM((slot_rows, taps), jnp.bfloat16),
            pltpu.VMEM((1, rows), jnp.int32),
            dma, dma,
            chunks, chunks, chunks, chunks, chunks,
            pltpu.VMEM((dp_count, slot_rows, taps), jnp.bfloat16),
            pltpu.VMEM((groups * rows, 2 * rows), jnp.bfloat16),
            pltpu.VMEM((8, rows), jnp.int32),
            pltpu.VMEM((8, rows), jnp.int32),
            pltpu.VMEM((rows, rows), jnp.bfloat16),
            pltpu.VMEM((rows, rows), jnp.bfloat16),
            dma((chunk_count,)), dma((chunk_count,)), dma((chunk_count,)),
            dma((dp_count,)), dma((dp_count,)),
            dma((chunk_count,)), dma((chunk_count,)),
            dma((chunk_count,)), dma((chunk_count,)),
            dma, dma,
        ],
        compiler_params=pltpu.CompilerParams(
            collective_id=0, has_side_effects=True, vmem_limit_bytes=62 * 1024 * 1024
        ),
        cost_estimate=pl.CostEstimate(
            flops=2 * 2 * rows * rows * channels * 16, bytes_accessed=6 * rows * channels, transcendentals=0
        ),
    )(gate, filt, doc_ids, loss_grad)


def solution(mesh):
    return jax.shard_map(
        functools.partial(body, dict(mesh.shape)),
        mesh=mesh,
        in_specs=(
            P("pipe", None, "dp", None),
            P("pipe", "dp", None),
            P(None, "dp"),
            P(None, "dp", None),
        ),
        out_specs=P("pipe", None, "dp", None),
        check_vma=False,
    )
```

```python
import functools

import jax
import jax.numpy as jnp
from jax import lax
from jax.experimental import pallas as pl
from jax.experimental.pallas import tpu as pltpu
from jax.sharding import PartitionSpec as P

MESH_ID = pl.DeviceIdType.MESH
CHUNK = 256
LAG = 5


def kernel(
    dp_count, pipe_count, lane_width, slot_groups,
    gate, filt_hbm, docs_hbm, loss, out,
    filt, docs, filt_sem, docs_sem, gbuf, inc, sbuf, halo, obuf, fall, table, docs_own, docs_next, mask_own, mask_next,
    gsem, lsem, osem, fsend, frecv, hsend, hrecv, psend, precv, dsend, drecv,
):
    chunk_count, rows, width = sbuf.shape
    groups = width // lane_width
    slots = groups // slot_groups
    stage = lax.axis_index("pipe")
    me = lax.axis_index("dp")
    is_last_stage = stage == pipe_count - 1
    not_last_stage = stage < pipe_count - 1
    has_below = stage > 0
    has_before = me > 0
    has_next = me < dp_count - 1

    def columns(j):
        return pl.ds(pl.multiple_of(j * width, width), width)

    def gate_copy(j):
        return pltpu.make_async_copy(gate.at[0, 0, :, columns(j)], gbuf.at[j], gsem.at[j])

    def loss_copy(j):
        return pltpu.make_async_copy(loss.at[0, :, columns(j)], inc.at[j], lsem.at[j])

    def out_copy(j):
        return pltpu.make_async_copy(obuf.at[j], out.at[0, 0, :, columns(j)], osem.at[j])

    def filter_copy(slot, peer):
        return pltpu.make_async_remote_copy(
            src_ref=filt, dst_ref=fall.at[slot], send_sem=fsend.at[peer], recv_sem=frecv.at[slot],
            device_id=(stage, peer), device_id_type=MESH_ID,
        )

    def halo_copy(j):
        return pltpu.make_async_remote_copy(
            src_ref=sbuf.at[j], dst_ref=halo.at[j], send_sem=hsend.at[j], recv_sem=hrecv.at[j],
            device_id=(stage, me - 1), device_id_type=MESH_ID,
        )

    def docs_copy():
        return pltpu.make_async_remote_copy(
            src_ref=docs_own, dst_ref=docs_next, send_sem=dsend, recv_sem=drecv,
            device_id=(stage, me - 1), device_id_type=MESH_ID,
        )

    def pipe_copy(j):
        return pltpu.make_async_remote_copy(
            src_ref=obuf.at[j], dst_ref=inc.at[j], send_sem=psend.at[j], recv_sem=precv.at[j],
            device_id=(stage - 1, me), device_id_type=MESH_ID,
        )

    def each(count, fn):
        def step(j, carry):
            fn(j)
            return carry
        lax.fori_loop(0, count, step, 0)

    load_filters = pltpu.make_async_copy(filt_hbm, filt, filt_sem)
    load_docs = pltpu.make_async_copy(docs_hbm, docs, docs_sem)
    load_filters.start()
    load_docs.start()
    each(chunk_count, lambda j: gate_copy(j).start())

    @pl.when(is_last_stage)
    def _():
        each(chunk_count, lambda j: loss_copy(j).start())

    barrier = pltpu.get_barrier_semaphore()

    def greet(k):
        pl.semaphore_signal(
            barrier, inc=1, device_id=(stage, lax.rem(me + k + 1, dp_count)), device_id_type=MESH_ID
        )

    each(dp_count - 1, greet)

    @pl.when(has_below)
    def _():
        pl.semaphore_signal(barrier, inc=1, device_id=(stage - 1, me), device_id_type=MESH_ID)

    @pl.when(not_last_stage)
    def _():
        pl.semaphore_signal(barrier, inc=1, device_id=(stage + 1, me), device_id_type=MESH_ID)

    load_filters.wait()
    load_docs.wait()
    docs_own[...] = jnp.broadcast_to(docs[...], docs_own.shape)
    fall[me] = filt[...]

    greeted = dp_count - 1 + has_below.astype(jnp.int32) + not_last_stage.astype(jnp.int32)
    pl.semaphore_wait(barrier, greeted)

    def send_filters(k):
        peer = lax.rem(me + k + 1, dp_count)
        filter_copy(me, peer).start()

    @pl.when(has_before)
    def _():
        docs_copy().start()

    each(dp_count - 1, send_filters)

    def scale(j):
        gate_copy(j).wait()

        @pl.when(is_last_stage)
        def _():
            loss_copy(j).wait()

        @pl.when(not_last_stage)
        def _():
            pltpu.make_async_remote_copy(
                src_ref=obuf.at[j], dst_ref=inc.at[j], send_sem=psend.at[j], recv_sem=precv.at[j],
                device_id=(stage + 1, me), device_id_type=MESH_ID,
            ).wait_recv()

        sbuf[j] = (gbuf[j].astype(jnp.float32) * inc[j].astype(jnp.float32)).astype(jnp.bfloat16)

        @pl.when(has_before)
        def _():
            halo_copy(j).start()

    @pl.when(is_last_stage)
    def _():
        each(chunk_count, scale)

    @pl.when(jnp.logical_not(has_next))
    def _():
        docs_next[...] = jnp.zeros_like(docs_next)

        def clear(j):
            halo[j] = jnp.zeros((rows, width), jnp.bfloat16)

        each(chunk_count, clear)

    @pl.when(has_next)
    def _():
        pltpu.make_async_remote_copy(
            src_ref=docs_own, dst_ref=docs_next, send_sem=dsend, recv_sem=drecv,
            device_id=(stage, me + 1), device_id_type=MESH_ID,
        ).wait_recv()

    at_row = lax.broadcasted_iota(jnp.int32, (rows, rows), 0)
    at_col = lax.broadcasted_iota(jnp.int32, (rows, rows), 1)
    own_cols = jnp.broadcast_to(docs_own[0:1, :], (rows, rows)).astype(jnp.float32)
    next_cols = jnp.broadcast_to(docs_next[0:1, :], (rows, rows)).astype(jnp.float32)
    own_rows = own_cols.T
    one, zero = jnp.float32(1.0), jnp.float32(0.0)
    mask_own[...] = jnp.where(
        jnp.logical_and(at_col >= at_row, own_rows == own_cols), one, zero
    ).astype(jnp.bfloat16)
    mask_next[...] = jnp.where(
        jnp.logical_and(at_col < at_row, own_rows == next_cols), one, zero
    ).astype(jnp.bfloat16)

    def make_table(j):
        for q in range(slots):
            slot = j * slots + q

            @pl.when(slot != me)
            def _():
                filter_copy(slot, slot).wait_recv()

        for q in range(slots):
            taps = fall[j * slots + q].astype(jnp.float32)
            for r in range(slot_groups):
                g = q * slot_groups + r
                spread = jnp.broadcast_to(taps[r : r + 1, :], (8, rows))
                first = pltpu.roll(spread, 0, 1, stride=1, stride_axis=0)
                pieces = [first] + [pltpu.roll(first, row, 1) for row in range(8, rows, 8)]
                turned = jnp.concatenate(pieces, axis=0).astype(jnp.bfloat16)
                table[j, g * rows : (g + 1) * rows, :rows] = turned * mask_own[...]
                table[j, g * rows : (g + 1) * rows, rows:] = turned * mask_next[...]

    def produce(j):
        @pl.when(has_next)
        def _():
            pltpu.make_async_remote_copy(
                src_ref=sbuf.at[j], dst_ref=halo.at[j], send_sem=hsend.at[j], recv_sem=hrecv.at[j],
                device_id=(stage, me + 1), device_id_type=MESH_ID,
            ).wait_recv()

        slab = jnp.concatenate([sbuf[j], halo[j]], axis=0)
        group_of = lax.broadcasted_iota(jnp.int32, (rows, width), 1) // lane_width
        total = inc[j].astype(jnp.float32)
        update = jnp.zeros((rows, width), jnp.float32)
        parts = jnp.dot(table[j], slab, preferred_element_type=jnp.float32)
        for g in range(groups):
            update = jnp.where(group_of == g, parts[g * rows : (g + 1) * rows, :], update)
        obuf[j] = (total + update).astype(jnp.bfloat16)

        @pl.when(has_below)
        def _():
            pipe_copy(j).start()

        out_copy(j).start()

    lag = LAG - (LAG - 1) * is_last_stage.astype(jnp.int32)

    def step(s):
        @pl.when(s < chunk_count)
        def _():
            make_table(s)

        @pl.when(jnp.logical_and(not_last_stage, s < chunk_count))
        def _():
            scale(s)

        @pl.when(s >= lag)
        def _():
            produce(s - lag)

    each(chunk_count + lag, step)

    def finish(j):
        out_copy(j).wait()

        @pl.when(has_below)
        def _():
            pipe_copy(j).wait_send()

        @pl.when(has_before)
        def _():
            halo_copy(j).wait_send()

    each(chunk_count, finish)

    @pl.when(has_before)
    def _():
        docs_copy().wait_send()

    each(dp_count - 1, lambda k: filter_copy(me, lax.rem(me + k + 1, dp_count)).wait_send())


def body(mesh_shape, gate, filters, doc_ids, loss_grad):
    dp_count, pipe_count = mesh_shape["dp"], mesh_shape["pipe"]
    _, _, rows, channels = gate.shape
    slot_groups, taps = filters.shape[1:]
    lane_width = channels // (slot_groups * dp_count)
    chunk_count = channels // CHUNK
    slot_rows = -(-slot_groups // 16) * 16
    filt = filters[0]
    if slot_rows != slot_groups:
        filt = jnp.pad(filt, ((0, slot_rows - slot_groups), (0, 0)))
    chunks = pltpu.VMEM((chunk_count, rows, CHUNK), jnp.bfloat16)
    groups = CHUNK // lane_width
    dma = pltpu.SemaphoreType.DMA
    return pl.pallas_call(
        functools.partial(kernel, dp_count, pipe_count, lane_width, slot_groups),
        out_shape=jax.ShapeDtypeStruct(gate.shape, jnp.bfloat16),
        in_specs=[
            pl.BlockSpec(memory_space=pl.ANY),
            pl.BlockSpec(memory_space=pl.ANY),
            pl.BlockSpec(memory_space=pl.ANY),
            pl.BlockSpec(memory_space=pl.ANY),
        ],
        out_specs=pl.BlockSpec(memory_space=pl.ANY),
        scratch_shapes=[
            pltpu.VMEM((slot_rows, taps), jnp.bfloat16),
            pltpu.VMEM((1, rows), jnp.int32),
            dma, dma,
            chunks, chunks, chunks, chunks, chunks,
            pltpu.VMEM((dp_count, slot_rows, taps), jnp.bfloat16),
            pltpu.VMEM((chunk_count, groups * rows, 2 * rows), jnp.bfloat16),
            pltpu.VMEM((8, rows), jnp.int32),
            pltpu.VMEM((8, rows), jnp.int32),
            pltpu.VMEM((rows, rows), jnp.bfloat16),
            pltpu.VMEM((rows, rows), jnp.bfloat16),
            dma((chunk_count,)), dma((chunk_count,)), dma((chunk_count,)),
            dma((dp_count,)), dma((dp_count,)),
            dma((chunk_count,)), dma((chunk_count,)),
            dma((chunk_count,)), dma((chunk_count,)),
            dma, dma,
        ],
        compiler_params=pltpu.CompilerParams(
            collective_id=0, has_side_effects=True, vmem_limit_bytes=62 * 1024 * 1024
        ),
        cost_estimate=pl.CostEstimate(
            flops=2 * 2 * rows * rows * channels * 16, bytes_accessed=6 * rows * channels, transcendentals=0
        ),
    )(gate, filt, doc_ids, loss_grad)


def solution(mesh):
    return jax.shard_map(
        functools.partial(body, dict(mesh.shape)),
        mesh=mesh,
        in_specs=(
            P("pipe", None, "dp", None),
            P("pipe", "dp", None),
            P(None, "dp"),
            P(None, "dp", None),
        ),
        out_specs=P("pipe", None, "dp", None),
        check_vma=False,
    )
```

```python
import functools

import jax
import jax.numpy as jnp
from jax import lax
from jax.experimental import pallas as pl
from jax.experimental.pallas import tpu as pltpu
from jax.sharding import PartitionSpec as P

MESH_ID = pl.DeviceIdType.MESH
CHUNK = 256
LAG = 4


def kernel(
    dp_count, pipe_count, lane_width, slot_groups,
    gate, filt_hbm, docs_hbm, loss, out,
    filt, docs, filt_sem, docs_sem, gbuf, inc, sbuf, halo, obuf, fall, table, docs_own, docs_next, mask_own, mask_next,
    gsem, lsem, osem, fsend, frecv, hsend, hrecv, psend, precv, dsend, drecv,
):
    chunk_count, rows, width = sbuf.shape
    groups = width // lane_width
    slots = groups // slot_groups
    stage = lax.axis_index("pipe")
    me = lax.axis_index("dp")
    is_last_stage = stage == pipe_count - 1
    not_last_stage = stage < pipe_count - 1
    has_below = stage > 0
    has_before = me > 0
    has_next = me < dp_count - 1

    def columns(j):
        return pl.ds(pl.multiple_of(j * width, width), width)

    def gate_copy(j):
        return pltpu.make_async_copy(gate.at[0, 0, :, columns(j)], gbuf.at[j], gsem.at[j])

    def loss_copy(j):
        return pltpu.make_async_copy(loss.at[0, :, columns(j)], inc.at[j], lsem.at[j])

    def out_copy(j):
        return pltpu.make_async_copy(obuf.at[j], out.at[0, 0, :, columns(j)], osem.at[j])

    def filter_copy(slot, peer):
        return pltpu.make_async_remote_copy(
            src_ref=filt, dst_ref=fall.at[slot], send_sem=fsend.at[peer], recv_sem=frecv.at[slot],
            device_id=(stage, peer), device_id_type=MESH_ID,
        )

    def halo_copy(j):
        return pltpu.make_async_remote_copy(
            src_ref=sbuf.at[j], dst_ref=halo.at[j], send_sem=hsend.at[j], recv_sem=hrecv.at[j],
            device_id=(stage, me - 1), device_id_type=MESH_ID,
        )

    def docs_copy():
        return pltpu.make_async_remote_copy(
            src_ref=docs_own, dst_ref=docs_next, send_sem=dsend, recv_sem=drecv,
            device_id=(stage, me - 1), device_id_type=MESH_ID,
        )

    def pipe_copy(j):
        return pltpu.make_async_remote_copy(
            src_ref=obuf.at[j], dst_ref=inc.at[j], send_sem=psend.at[j], recv_sem=precv.at[j],
            device_id=(stage - 1, me), device_id_type=MESH_ID,
        )

    def each(count, fn):
        def step(j, carry):
            fn(j)
            return carry
        lax.fori_loop(0, count, step, 0)

    load_filters = pltpu.make_async_copy(filt_hbm, filt, filt_sem)
    load_docs = pltpu.make_async_copy(docs_hbm, docs, docs_sem)
    load_filters.start()
    load_docs.start()
    each(chunk_count, lambda j: gate_copy(j).start())

    @pl.when(is_last_stage)
    def _():
        each(chunk_count, lambda j: loss_copy(j).start())

    barrier = pltpu.get_barrier_semaphore()

    def greet(k):
        pl.semaphore_signal(
            barrier, inc=1, device_id=(stage, lax.rem(me + k + 1, dp_count)), device_id_type=MESH_ID
        )

    each(dp_count - 1, greet)

    @pl.when(has_below)
    def _():
        pl.semaphore_signal(barrier, inc=1, device_id=(stage - 1, me), device_id_type=MESH_ID)

    @pl.when(not_last_stage)
    def _():
        pl.semaphore_signal(barrier, inc=1, device_id=(stage + 1, me), device_id_type=MESH_ID)

    load_filters.wait()
    load_docs.wait()
    docs_own[...] = jnp.broadcast_to(docs[...], docs_own.shape)
    fall[me] = filt[...]

    greeted = dp_count - 1 + has_below.astype(jnp.int32) + not_last_stage.astype(jnp.int32)
    pl.semaphore_wait(barrier, greeted)

    def send_filters(k):
        peer = lax.rem(me + k + 1, dp_count)
        filter_copy(me, peer).start()

    @pl.when(has_before)
    def _():
        docs_copy().start()

    each(dp_count - 1, send_filters)

    def scale(j):
        gate_copy(j).wait()

        @pl.when(is_last_stage)
        def _():
            loss_copy(j).wait()

        @pl.when(not_last_stage)
        def _():
            pltpu.make_async_remote_copy(
                src_ref=obuf.at[j], dst_ref=inc.at[j], send_sem=psend.at[j], recv_sem=precv.at[j],
                device_id=(stage + 1, me), device_id_type=MESH_ID,
            ).wait_recv()

        sbuf[j] = (gbuf[j].astype(jnp.float32) * inc[j].astype(jnp.float32)).astype(jnp.bfloat16)

        @pl.when(has_before)
        def _():
            halo_copy(j).start()

    @pl.when(is_last_stage)
    def _():
        each(chunk_count, scale)

    @pl.when(jnp.logical_not(has_next))
    def _():
        docs_next[...] = jnp.zeros_like(docs_next)

        def clear(j):
            halo[j] = jnp.zeros((rows, width), jnp.bfloat16)

        each(chunk_count, clear)

    @pl.when(has_next)
    def _():
        pltpu.make_async_remote_copy(
            src_ref=docs_own, dst_ref=docs_next, send_sem=dsend, recv_sem=drecv,
            device_id=(stage, me + 1), device_id_type=MESH_ID,
        ).wait_recv()

    at_row = lax.broadcasted_iota(jnp.int32, (rows, rows), 0)
    at_col = lax.broadcasted_iota(jnp.int32, (rows, rows), 1)
    own_cols = jnp.broadcast_to(docs_own[0:1, :], (rows, rows)).astype(jnp.float32)
    next_cols = jnp.broadcast_to(docs_next[0:1, :], (rows, rows)).astype(jnp.float32)
    own_rows = own_cols.T
    one, zero = jnp.float32(1.0), jnp.float32(0.0)
    mask_own[...] = jnp.where(
        jnp.logical_and(at_col >= at_row, own_rows == own_cols), one, zero
    ).astype(jnp.bfloat16)
    mask_next[...] = jnp.where(
        jnp.logical_and(at_col < at_row, own_rows == next_cols), one, zero
    ).astype(jnp.bfloat16)

    def make_table(j):
        for q in range(slots):
            slot = j * slots + q

            @pl.when(slot != me)
            def _():
                filter_copy(slot, slot).wait_recv()

        for q in range(slots):
            taps = fall[j * slots + q].astype(jnp.float32)
            for r in range(slot_groups):
                g = q * slot_groups + r
                spread = jnp.broadcast_to(taps[r : r + 1, :], (rows, rows))
                turned = pltpu.roll(spread, 0, 1, stride=1, stride_axis=0).astype(jnp.bfloat16)
                table[j, g * rows : (g + 1) * rows, :rows] = turned * mask_own[...]
                table[j, g * rows : (g + 1) * rows, rows:] = turned * mask_next[...]

    def produce(j):
        @pl.when(has_next)
        def _():
            pltpu.make_async_remote_copy(
                src_ref=sbuf.at[j], dst_ref=halo.at[j], send_sem=hsend.at[j], recv_sem=hrecv.at[j],
                device_id=(stage, me + 1), device_id_type=MESH_ID,
            ).wait_recv()

        slab = jnp.concatenate([sbuf[j], halo[j]], axis=0)
        group_of = lax.broadcasted_iota(jnp.int32, (rows, width), 1) // lane_width
        total = inc[j].astype(jnp.float32)
        update = jnp.zeros((rows, width), jnp.float32)
        parts = jnp.dot(table[j], slab, preferred_element_type=jnp.float32)
        for g in range(groups):
            update = jnp.where(group_of == g, parts[g * rows : (g + 1) * rows, :], update)
        obuf[j] = (total + update).astype(jnp.bfloat16)

        @pl.when(has_below)
        def _():
            pipe_copy(j).start()

        out_copy(j).start()

    lag = LAG * not_last_stage.astype(jnp.int32)

    def step(s):
        @pl.when(s < chunk_count)
        def _():
            make_table(s)

        @pl.when(jnp.logical_and(not_last_stage, s < chunk_count))
        def _():
            scale(s)

        @pl.when(s >= lag)
        def _():
            produce(s - lag)

    each(chunk_count + lag, step)

    def finish(j):
        out_copy(j).wait()

        @pl.when(has_below)
        def _():
            pipe_copy(j).wait_send()

        @pl.when(has_before)
        def _():
            halo_copy(j).wait_send()

    each(chunk_count, finish)

    @pl.when(has_before)
    def _():
        docs_copy().wait_send()

    each(dp_count - 1, lambda k: filter_copy(me, lax.rem(me + k + 1, dp_count)).wait_send())


def body(mesh_shape, gate, filters, doc_ids, loss_grad):
    dp_count, pipe_count = mesh_shape["dp"], mesh_shape["pipe"]
    _, _, rows, channels = gate.shape
    slot_groups, taps = filters.shape[1:]
    lane_width = channels // (slot_groups * dp_count)
    chunk_count = channels // CHUNK
    slot_rows = -(-slot_groups // 16) * 16
    filt = filters[0]
    if slot_rows != slot_groups:
        filt = jnp.pad(filt, ((0, slot_rows - slot_groups), (0, 0)))
    chunks = pltpu.VMEM((chunk_count, rows, CHUNK), jnp.bfloat16)
    groups = CHUNK // lane_width
    dma = pltpu.SemaphoreType.DMA
    return pl.pallas_call(
        functools.partial(kernel, dp_count, pipe_count, lane_width, slot_groups),
        out_shape=jax.ShapeDtypeStruct(gate.shape, jnp.bfloat16),
        in_specs=[
            pl.BlockSpec(memory_space=pl.ANY),
            pl.BlockSpec(memory_space=pl.ANY),
            pl.BlockSpec(memory_space=pl.ANY),
            pl.BlockSpec(memory_space=pl.ANY),
        ],
        out_specs=pl.BlockSpec(memory_space=pl.ANY),
        scratch_shapes=[
            pltpu.VMEM((slot_rows, taps), jnp.bfloat16),
            pltpu.VMEM((1, rows), jnp.int32),
            dma, dma,
            chunks, chunks, chunks, chunks, chunks,
            pltpu.VMEM((dp_count, slot_rows, taps), jnp.bfloat16),
            pltpu.VMEM((chunk_count, groups * rows, 2 * rows), jnp.bfloat16),
            pltpu.VMEM((8, rows), jnp.int32),
            pltpu.VMEM((8, rows), jnp.int32),
            pltpu.VMEM((rows, rows), jnp.bfloat16),
            pltpu.VMEM((rows, rows), jnp.bfloat16),
            dma((chunk_count,)), dma((chunk_count,)), dma((chunk_count,)),
            dma((dp_count,)), dma((dp_count,)),
            dma((chunk_count,)), dma((chunk_count,)),
            dma((chunk_count,)), dma((chunk_count,)),
            dma, dma,
        ],
        compiler_params=pltpu.CompilerParams(
            collective_id=0, has_side_effects=True, vmem_limit_bytes=62 * 1024 * 1024
        ),
        cost_estimate=pl.CostEstimate(
            flops=2 * 2 * rows * rows * channels * 16, bytes_accessed=6 * rows * channels, transcendentals=0
        ),
    )(gate, filt, doc_ids, loss_grad)


def solution(mesh):
    return jax.shard_map(
        functools.partial(body, dict(mesh.shape)),
        mesh=mesh,
        in_specs=(
            P("pipe", None, "dp", None),
            P("pipe", "dp", None),
            P(None, "dp"),
            P(None, "dp", None),
        ),
        out_specs=P("pipe", None, "dp", None),
        check_vma=False,
    )
```

```python
import functools

import jax
import jax.numpy as jnp
from jax import lax
from jax.experimental import pallas as pl
from jax.experimental.pallas import tpu as pltpu
from jax.sharding import PartitionSpec as P

MESH_ID = pl.DeviceIdType.MESH
CHUNK = 256
LAG = 4
DOT_GROUPS = 4


def kernel(
    dp_count, pipe_count, lane_width, slot_groups,
    gate, filt_hbm, docs_hbm, loss, out,
    filt, docs, filt_sem, docs_sem, gbuf, inc, sbuf, halo, obuf, fall, docs_own, docs_next, mask_own, mask_next,
    gsem, lsem, osem, fsend, frecv, hsend, hrecv, psend, precv, dsend, drecv,
):
    chunk_count, rows, width = sbuf.shape
    groups = width // lane_width
    slots = groups // slot_groups
    stage = lax.axis_index("pipe")
    me = lax.axis_index("dp")
    is_last_stage = stage == pipe_count - 1
    not_last_stage = stage < pipe_count - 1
    has_below = stage > 0
    has_before = me > 0
    has_next = me < dp_count - 1

    def columns(j):
        return pl.ds(pl.multiple_of(j * width, width), width)

    def gate_copy(j):
        return pltpu.make_async_copy(gate.at[0, 0, :, columns(j)], gbuf.at[j], gsem.at[j])

    def loss_copy(j):
        return pltpu.make_async_copy(loss.at[0, :, columns(j)], inc.at[j], lsem.at[j])

    def out_copy(j):
        return pltpu.make_async_copy(obuf.at[j], out.at[0, 0, :, columns(j)], osem.at[j])

    def filter_copy(slot, peer):
        return pltpu.make_async_remote_copy(
            src_ref=filt, dst_ref=fall.at[slot], send_sem=fsend.at[peer], recv_sem=frecv.at[slot],
            device_id=(stage, peer), device_id_type=MESH_ID,
        )

    def halo_copy(j):
        return pltpu.make_async_remote_copy(
            src_ref=sbuf.at[j], dst_ref=halo.at[j], send_sem=hsend.at[j], recv_sem=hrecv.at[j],
            device_id=(stage, me - 1), device_id_type=MESH_ID,
        )

    def docs_copy():
        return pltpu.make_async_remote_copy(
            src_ref=docs_own, dst_ref=docs_next, send_sem=dsend, recv_sem=drecv,
            device_id=(stage, me - 1), device_id_type=MESH_ID,
        )

    def pipe_copy(j):
        return pltpu.make_async_remote_copy(
            src_ref=obuf.at[j], dst_ref=inc.at[j], send_sem=psend.at[j], recv_sem=precv.at[j],
            device_id=(stage - 1, me), device_id_type=MESH_ID,
        )

    def each(count, fn):
        def step(j, carry):
            fn(j)
            return carry
        lax.fori_loop(0, count, step, 0)

    load_filters = pltpu.make_async_copy(filt_hbm, filt, filt_sem)
    load_docs = pltpu.make_async_copy(docs_hbm, docs, docs_sem)
    load_filters.start()
    load_docs.start()
    each(chunk_count, lambda j: gate_copy(j).start())

    @pl.when(is_last_stage)
    def _():
        each(chunk_count, lambda j: loss_copy(j).start())

    barrier = pltpu.get_barrier_semaphore()

    def greet(k):
        pl.semaphore_signal(
            barrier, inc=1, device_id=(stage, lax.rem(me + k + 1, dp_count)), device_id_type=MESH_ID
        )

    each(dp_count - 1, greet)

    @pl.when(has_below)
    def _():
        pl.semaphore_signal(barrier, inc=1, device_id=(stage - 1, me), device_id_type=MESH_ID)

    @pl.when(not_last_stage)
    def _():
        pl.semaphore_signal(barrier, inc=1, device_id=(stage + 1, me), device_id_type=MESH_ID)

    load_filters.wait()
    load_docs.wait()
    docs_own[...] = jnp.broadcast_to(docs[...], docs_own.shape)
    fall[me] = filt[...]

    greeted = dp_count - 1 + has_below.astype(jnp.int32) + not_last_stage.astype(jnp.int32)
    pl.semaphore_wait(barrier, greeted)

    def send_filters(k):
        peer = lax.rem(me + k + 1, dp_count)
        filter_copy(me, peer).start()

    @pl.when(has_before)
    def _():
        docs_copy().start()

    each(dp_count - 1, send_filters)

    def scale(j):
        gate_copy(j).wait()

        @pl.when(is_last_stage)
        def _():
            loss_copy(j).wait()

        @pl.when(not_last_stage)
        def _():
            pltpu.make_async_remote_copy(
                src_ref=obuf.at[j], dst_ref=inc.at[j], send_sem=psend.at[j], recv_sem=precv.at[j],
                device_id=(stage + 1, me), device_id_type=MESH_ID,
            ).wait_recv()

        sbuf[j] = (gbuf[j].astype(jnp.float32) * inc[j].astype(jnp.float32)).astype(jnp.bfloat16)

        @pl.when(has_before)
        def _():
            halo_copy(j).start()

    @pl.when(is_last_stage)
    def _():
        each(chunk_count, scale)

    @pl.when(jnp.logical_not(has_next))
    def _():
        docs_next[...] = jnp.zeros_like(docs_next)

        def clear(j):
            halo[j] = jnp.zeros((rows, width), jnp.bfloat16)

        each(chunk_count, clear)

    @pl.when(has_next)
    def _():
        pltpu.make_async_remote_copy(
            src_ref=docs_own, dst_ref=docs_next, send_sem=dsend, recv_sem=drecv,
            device_id=(stage, me + 1), device_id_type=MESH_ID,
        ).wait_recv()

    at_row = lax.broadcasted_iota(jnp.int32, (rows, rows), 0)
    at_col = lax.broadcasted_iota(jnp.int32, (rows, rows), 1)
    own_cols = jnp.broadcast_to(docs_own[0:1, :], (rows, rows)).astype(jnp.float32)
    next_cols = jnp.broadcast_to(docs_next[0:1, :], (rows, rows)).astype(jnp.float32)
    own_rows = own_cols.T
    one, zero = jnp.float32(1.0), jnp.float32(0.0)
    mask_own[...] = jnp.where(
        jnp.logical_and(at_col >= at_row, own_rows == own_cols), one, zero
    ).astype(jnp.bfloat16)
    mask_next[...] = jnp.where(
        jnp.logical_and(at_col < at_row, own_rows == next_cols), one, zero
    ).astype(jnp.bfloat16)

    def wait_filters(j):
        for q in range(slots):
            slot = j * slots + q

            @pl.when(slot != me)
            def _():
                filter_copy(slot, slot).wait_recv()


    def produce(j):
        wait_filters(j)

        @pl.when(has_next)
        def _():
            pltpu.make_async_remote_copy(
                src_ref=sbuf.at[j], dst_ref=halo.at[j], send_sem=hsend.at[j], recv_sem=hrecv.at[j],
                device_id=(stage, me + 1), device_id_type=MESH_ID,
            ).wait_recv()

        slab = jnp.concatenate([sbuf[j], halo[j]], axis=0)
        group_of = lax.broadcasted_iota(jnp.int32, (rows, width), 1) // lane_width
        total = inc[j].astype(jnp.float32)
        update = jnp.zeros((rows, width), jnp.float32)
        taps = [fall[j * slots + q].astype(jnp.float32) for q in range(slots)]
        for start in range(0, groups, DOT_GROUPS):
            tables = []
            for g in range(start, start + DOT_GROUPS):
                q, r = divmod(g, slot_groups)
                spread = jnp.broadcast_to(taps[q][r : r + 1, :], (rows, rows))
                turned = pltpu.roll(spread, 0, 1, stride=1, stride_axis=0).astype(jnp.bfloat16)
                tables.append(
                    jnp.concatenate([turned * mask_own[...], turned * mask_next[...]], axis=1)
                )
            parts = jnp.dot(
                jnp.concatenate(tables, axis=0), slab, preferred_element_type=jnp.float32
            )
            for k in range(DOT_GROUPS):
                update = jnp.where(
                    group_of == start + k, parts[k * rows : (k + 1) * rows, :], update
                )
        obuf[j] = (total + update).astype(jnp.bfloat16)

        @pl.when(has_below)
        def _():
            pipe_copy(j).start()

        out_copy(j).start()

    lag = LAG * not_last_stage.astype(jnp.int32)

    def step(s):
        @pl.when(jnp.logical_and(not_last_stage, s < chunk_count))
        def _():
            scale(s)

        @pl.when(s >= lag)
        def _():
            produce(s - lag)

    each(chunk_count + lag, step)

    def finish(j):
        out_copy(j).wait()

        @pl.when(has_below)
        def _():
            pipe_copy(j).wait_send()

        @pl.when(has_before)
        def _():
            halo_copy(j).wait_send()

    each(chunk_count, finish)

    @pl.when(has_before)
    def _():
        docs_copy().wait_send()

    each(dp_count - 1, lambda k: filter_copy(me, lax.rem(me + k + 1, dp_count)).wait_send())


def body(mesh_shape, gate, filters, doc_ids, loss_grad):
    dp_count, pipe_count = mesh_shape["dp"], mesh_shape["pipe"]
    _, _, rows, channels = gate.shape
    slot_groups, taps = filters.shape[1:]
    lane_width = channels // (slot_groups * dp_count)
    chunk_count = channels // CHUNK
    slot_rows = -(-slot_groups // 16) * 16
    filt = filters[0]
    if slot_rows != slot_groups:
        filt = jnp.pad(filt, ((0, slot_rows - slot_groups), (0, 0)))
    chunks = pltpu.VMEM((chunk_count, rows, CHUNK), jnp.bfloat16)
    dma = pltpu.SemaphoreType.DMA
    return pl.pallas_call(
        functools.partial(kernel, dp_count, pipe_count, lane_width, slot_groups),
        out_shape=jax.ShapeDtypeStruct(gate.shape, jnp.bfloat16),
        in_specs=[
            pl.BlockSpec(memory_space=pl.ANY),
            pl.BlockSpec(memory_space=pl.ANY),
            pl.BlockSpec(memory_space=pl.ANY),
            pl.BlockSpec(memory_space=pl.ANY),
        ],
        out_specs=pl.BlockSpec(memory_space=pl.ANY),
        scratch_shapes=[
            pltpu.VMEM((slot_rows, taps), jnp.bfloat16),
            pltpu.VMEM((1, rows), jnp.int32),
            dma, dma,
            chunks, chunks, chunks, chunks, chunks,
            pltpu.VMEM((dp_count, slot_rows, taps), jnp.bfloat16),
            pltpu.VMEM((8, rows), jnp.int32),
            pltpu.VMEM((8, rows), jnp.int32),
            pltpu.VMEM((rows, rows), jnp.bfloat16),
            pltpu.VMEM((rows, rows), jnp.bfloat16),
            dma((chunk_count,)), dma((chunk_count,)), dma((chunk_count,)),
            dma((dp_count,)), dma((dp_count,)),
            dma((chunk_count,)), dma((chunk_count,)),
            dma((chunk_count,)), dma((chunk_count,)),
            dma, dma,
        ],
        compiler_params=pltpu.CompilerParams(
            collective_id=0, has_side_effects=True, vmem_limit_bytes=62 * 1024 * 1024
        ),
        cost_estimate=pl.CostEstimate(
            flops=2 * 2 * rows * rows * channels * 16, bytes_accessed=6 * rows * channels, transcendentals=0
        ),
    )(gate, filt, doc_ids, loss_grad)


def solution(mesh):
    return jax.shard_map(
        functools.partial(body, dict(mesh.shape)),
        mesh=mesh,
        in_specs=(
            P("pipe", None, "dp", None),
            P("pipe", "dp", None),
            P(None, "dp"),
            P(None, "dp", None),
        ),
        out_specs=P("pipe", None, "dp", None),
        check_vma=False,
    )
```

```python
import functools

import jax
import jax.numpy as jnp
from jax import lax
from jax.experimental import pallas as pl
from jax.experimental.pallas import tpu as pltpu
from jax.sharding import PartitionSpec as P

MESH_ID = pl.DeviceIdType.MESH
CHUNK = 256
LAG = 5
PLANE = 4
DOT_GROUPS = 4


def kernel(
    dp_count, pipe_count, lane_width, slot_groups,
    gate, filt_hbm, docs_hbm, loss, out,
    filt, docs, filt_sem, docs_sem, gbuf, inc, sbuf, halo, obuf, fall, docs_own, docs_next, mask_own, mask_next,
    gsem, lsem, osem, fsend, frecv, hsend, hrecv, psend, precv, dsend, drecv,
):
    chunk_count, rows, width = sbuf.shape
    groups = width // lane_width
    slots = groups // slot_groups
    stage = lax.axis_index("pipe")
    me = lax.axis_index("dp")
    is_last_stage = stage == pipe_count - 1
    not_last_stage = stage < pipe_count - 1
    has_below = stage > 0
    has_before = me > 0
    has_next = me < dp_count - 1
    planes = dp_count // PLANE
    plane, place = me // PLANE, lax.rem(me, PLANE)
    plane_after, plane_before = plane < planes - 1, plane > 0
    next_apart = jnp.logical_and(place == PLANE - 1, plane_after)
    before_apart = jnp.logical_and(place == 0, plane_before)

    def columns(j):
        return pl.ds(pl.multiple_of(j * width, width), width)

    def gate_copy(j):
        return pltpu.make_async_copy(gate.at[0, 0, :, columns(j)], gbuf.at[j], gsem.at[j])

    def loss_copy(j):
        return pltpu.make_async_copy(loss.at[0, :, columns(j)], inc.at[j], lsem.at[j])

    def out_copy(j):
        return pltpu.make_async_copy(obuf.at[j], out.at[0, 0, :, columns(j)], osem.at[j])

    def filter_copy(slot, peer, way):
        return pltpu.make_async_remote_copy(
            src_ref=fall.at[slot], dst_ref=fall.at[slot],
            send_sem=fsend.at[slot // PLANE, way], recv_sem=frecv.at[slot],
            device_id=(stage, peer), device_id_type=MESH_ID,
        )

    def beside(k):
        return plane * PLANE + lax.rem(place + k, PLANE)

    def each_forward(p, act):
        slot = p * PLANE + place

        @pl.when(jnp.logical_and(p <= plane, plane_after))
        def _():
            act(filter_copy(slot, me + PLANE, 0))

        @pl.when(jnp.logical_and(p >= plane, plane_before))
        def _():
            act(filter_copy(slot, me - PLANE, 1))

        for k in range(1, PLANE):
            act(filter_copy(slot, beside(k), 1 + k))

    def forward(p):
        filter_copy(p * PLANE + place, beside(1), 0).wait_recv()
        each_forward(p, lambda copy: copy.start())

    def halo_copy(j):
        return pltpu.make_async_remote_copy(
            src_ref=sbuf.at[j], dst_ref=halo.at[j], send_sem=hsend.at[j], recv_sem=hrecv.at[j],
            device_id=(stage, me - 1), device_id_type=MESH_ID,
        )

    def docs_copy():
        return pltpu.make_async_remote_copy(
            src_ref=docs_own, dst_ref=docs_next, send_sem=dsend, recv_sem=drecv,
            device_id=(stage, me - 1), device_id_type=MESH_ID,
        )

    def pipe_copy(j):
        return pltpu.make_async_remote_copy(
            src_ref=obuf.at[j], dst_ref=inc.at[j], send_sem=psend.at[j], recv_sem=precv.at[j],
            device_id=(stage - 1, me), device_id_type=MESH_ID,
        )

    def each(count, fn):
        def step(j, carry):
            fn(j)
            return carry
        lax.fori_loop(0, count, step, 0)

    load_filters = pltpu.make_async_copy(filt_hbm, filt, filt_sem)
    load_docs = pltpu.make_async_copy(docs_hbm, docs, docs_sem)
    load_filters.start()
    load_docs.start()
    each(chunk_count, lambda j: gate_copy(j).start())

    @pl.when(is_last_stage)
    def _():
        each(chunk_count, lambda j: loss_copy(j).start())

    barrier = pltpu.get_barrier_semaphore()

    def greet(peer):
        pl.semaphore_signal(barrier, inc=1, device_id=(stage, peer), device_id_type=MESH_ID)

    for k in range(1, PLANE):
        greet(beside(k))
    for near, step_by in (
        (plane_after, PLANE), (plane_before, -PLANE), (next_apart, 1), (before_apart, -1)
    ):
        @pl.when(near)
        def _(step_by=step_by):
            greet(me + step_by)

    @pl.when(has_below)
    def _():
        pl.semaphore_signal(barrier, inc=1, device_id=(stage - 1, me), device_id_type=MESH_ID)

    @pl.when(not_last_stage)
    def _():
        pl.semaphore_signal(barrier, inc=1, device_id=(stage + 1, me), device_id_type=MESH_ID)

    load_filters.wait()
    load_docs.wait()
    docs_own[...] = jnp.broadcast_to(docs[...], docs_own.shape)
    fall[me] = filt[...]

    greeted = PLANE - 1
    for near in (plane_after, plane_before, next_apart, before_apart, has_below, not_last_stage):
        greeted = greeted + near.astype(jnp.int32)
    pl.semaphore_wait(barrier, greeted)

    @pl.when(has_before)
    def _():
        docs_copy().start()

    each_forward(plane, lambda copy: copy.start())

    def scale(j):
        gate_copy(j).wait()

        @pl.when(is_last_stage)
        def _():
            loss_copy(j).wait()

        @pl.when(not_last_stage)
        def _():
            pltpu.make_async_remote_copy(
                src_ref=obuf.at[j], dst_ref=inc.at[j], send_sem=psend.at[j], recv_sem=precv.at[j],
                device_id=(stage + 1, me), device_id_type=MESH_ID,
            ).wait_recv()

        sbuf[j] = (gbuf[j].astype(jnp.float32) * inc[j].astype(jnp.float32)).astype(jnp.bfloat16)

        @pl.when(has_before)
        def _():
            halo_copy(j).start()

    @pl.when(is_last_stage)
    def _():
        each(chunk_count, scale)

    @pl.when(jnp.logical_not(has_next))
    def _():
        docs_next[...] = jnp.zeros_like(docs_next)

        def clear(j):
            halo[j] = jnp.zeros((rows, width), jnp.bfloat16)

        each(chunk_count, clear)

    @pl.when(has_next)
    def _():
        pltpu.make_async_remote_copy(
            src_ref=docs_own, dst_ref=docs_next, send_sem=dsend, recv_sem=drecv,
            device_id=(stage, me + 1), device_id_type=MESH_ID,
        ).wait_recv()

    at_row = lax.broadcasted_iota(jnp.int32, (rows, rows), 0)
    at_col = lax.broadcasted_iota(jnp.int32, (rows, rows), 1)
    own_cols = jnp.broadcast_to(docs_own[0:1, :], (rows, rows)).astype(jnp.float32)
    next_cols = jnp.broadcast_to(docs_next[0:1, :], (rows, rows)).astype(jnp.float32)
    own_rows = own_cols.T
    one, zero = jnp.float32(1.0), jnp.float32(0.0)
    mask_own[...] = jnp.where(
        jnp.logical_and(at_col >= at_row, own_rows == own_cols), one, zero
    ).astype(jnp.bfloat16)
    mask_next[...] = jnp.where(
        jnp.logical_and(at_col < at_row, own_rows == next_cols), one, zero
    ).astype(jnp.bfloat16)

    def wait_filters(j):
        for q in range(slots):
            slot = j * slots + q

            @pl.when(lax.rem(slot, PLANE) != place)
            def _():
                filter_copy(slot, beside(1), 0).wait_recv()


    def produce(j):
        wait_filters(j)

        @pl.when(has_next)
        def _():
            pltpu.make_async_remote_copy(
                src_ref=sbuf.at[j], dst_ref=halo.at[j], send_sem=hsend.at[j], recv_sem=hrecv.at[j],
                device_id=(stage, me + 1), device_id_type=MESH_ID,
            ).wait_recv()

        slab = jnp.concatenate([sbuf[j], halo[j]], axis=0)
        group_of = lax.broadcasted_iota(jnp.int32, (rows, width), 1) // lane_width
        total = inc[j].astype(jnp.float32)
        update = jnp.zeros((rows, width), jnp.float32)
        taps = [fall[j * slots + q].astype(jnp.float32) for q in range(slots)]
        for start in range(0, groups, DOT_GROUPS):
            tables = []
            for g in range(start, start + DOT_GROUPS):
                q, r = divmod(g, slot_groups)
                spread = jnp.broadcast_to(taps[q][r : r + 1, :], (rows, rows))
                turned = pltpu.roll(spread, 0, 1, stride=1, stride_axis=0).astype(jnp.bfloat16)
                tables.append(
                    jnp.concatenate([turned * mask_own[...], turned * mask_next[...]], axis=1)
                )
            parts = jnp.dot(
                jnp.concatenate(tables, axis=0), slab, preferred_element_type=jnp.float32
            )
            for k in range(DOT_GROUPS):
                update = jnp.where(
                    group_of == start + k, parts[k * rows : (k + 1) * rows, :], update
                )
        obuf[j] = (total + update).astype(jnp.bfloat16)

        @pl.when(has_below)
        def _():
            pipe_copy(j).start()

        out_copy(j).start()

    lag = LAG * not_last_stage.astype(jnp.int32)

    @pl.when(plane_before)
    def _():
        forward(0)

    plane_steps = PLANE // slots

    def step(s):
        upcoming = s // plane_steps + 1

        @pl.when(jnp.logical_and(
            jnp.logical_and(lax.rem(s, plane_steps) == 0, upcoming < planes), upcoming != plane
        ))
        def _():
            forward(upcoming)

        @pl.when(jnp.logical_and(not_last_stage, s < chunk_count))
        def _():
            scale(s)

        @pl.when(s >= lag)
        def _():
            produce(s - lag)

    each(chunk_count + lag, step)

    def finish(j):
        out_copy(j).wait()

        @pl.when(has_below)
        def _():
            pipe_copy(j).wait_send()

        @pl.when(has_before)
        def _():
            halo_copy(j).wait_send()

    each(chunk_count, finish)

    @pl.when(has_before)
    def _():
        docs_copy().wait_send()

    each(planes, lambda p: each_forward(p, lambda copy: copy.wait_send()))


def body(mesh_shape, gate, filters, doc_ids, loss_grad):
    dp_count, pipe_count = mesh_shape["dp"], mesh_shape["pipe"]
    _, _, rows, channels = gate.shape
    slot_groups, taps = filters.shape[1:]
    lane_width = channels // (slot_groups * dp_count)
    chunk_count = channels // CHUNK
    slot_rows = -(-slot_groups // 16) * 16
    filt = filters[0]
    if slot_rows != slot_groups:
        filt = jnp.pad(filt, ((0, slot_rows - slot_groups), (0, 0)))
    chunks = pltpu.VMEM((chunk_count, rows, CHUNK), jnp.bfloat16)
    dma = pltpu.SemaphoreType.DMA
    return pl.pallas_call(
        functools.partial(kernel, dp_count, pipe_count, lane_width, slot_groups),
        out_shape=jax.ShapeDtypeStruct(gate.shape, jnp.bfloat16),
        in_specs=[
            pl.BlockSpec(memory_space=pl.ANY),
            pl.BlockSpec(memory_space=pl.ANY),
            pl.BlockSpec(memory_space=pl.ANY),
            pl.BlockSpec(memory_space=pl.ANY),
        ],
        out_specs=pl.BlockSpec(memory_space=pl.ANY),
        scratch_shapes=[
            pltpu.VMEM((slot_rows, taps), jnp.bfloat16),
            pltpu.VMEM((1, rows), jnp.int32),
            dma, dma,
            chunks, chunks, chunks, chunks, chunks,
            pltpu.VMEM((dp_count, slot_rows, taps), jnp.bfloat16),
            pltpu.VMEM((8, rows), jnp.int32),
            pltpu.VMEM((8, rows), jnp.int32),
            pltpu.VMEM((rows, rows), jnp.bfloat16),
            pltpu.VMEM((rows, rows), jnp.bfloat16),
            dma((chunk_count,)), dma((chunk_count,)), dma((chunk_count,)),
            dma((dp_count // PLANE, PLANE + 1)), dma((dp_count,)),
            dma((chunk_count,)), dma((chunk_count,)),
            dma((chunk_count,)), dma((chunk_count,)),
            dma, dma,
        ],
        compiler_params=pltpu.CompilerParams(
            collective_id=0, has_side_effects=True, vmem_limit_bytes=62 * 1024 * 1024
        ),
        cost_estimate=pl.CostEstimate(
            flops=2 * 2 * rows * rows * channels * 16, bytes_accessed=6 * rows * channels, transcendentals=0
        ),
    )(gate, filt, doc_ids, loss_grad)


def solution(mesh):
    return jax.shard_map(
        functools.partial(body, dict(mesh.shape)),
        mesh=mesh,
        in_specs=(
            P("pipe", None, "dp", None),
            P("pipe", "dp", None),
            P(None, "dp"),
            P(None, "dp", None),
        ),
        out_specs=P("pipe", None, "dp", None),
        check_vma=False,
    )
```

```python
import functools

import jax
import jax.numpy as jnp
from jax import lax
from jax.experimental import pallas as pl
from jax.experimental.pallas import tpu as pltpu
from jax.sharding import PartitionSpec as P

MESH_ID = pl.DeviceIdType.MESH
CHUNK = 256
LAG = 4
AHEAD = 5
DOT_GROUPS = 4


def kernel(
    dp_count, pipe_count, lane_width, slot_groups,
    gate, filt_hbm, docs_hbm, loss, out,
    filt, docs, filt_sem, docs_sem, gbuf, inc, sbuf, halo, obuf, fall, docs_own, docs_next, mask_own, mask_next,
    gsem, lsem, osem, fsend, frecv, hsend, hrecv, psend, precv, dsend, drecv,
):
    chunk_count, rows, width = sbuf.shape
    groups = width // lane_width
    slots = groups // slot_groups
    stage = lax.axis_index("pipe")
    me = lax.axis_index("dp")
    is_last_stage = stage == pipe_count - 1
    not_last_stage = stage < pipe_count - 1
    has_below = stage > 0
    has_before = me > 0
    has_next = me < dp_count - 1

    def columns(j):
        return pl.ds(pl.multiple_of(j * width, width), width)

    def gate_copy(j):
        return pltpu.make_async_copy(gate.at[0, 0, :, columns(j)], gbuf.at[j], gsem.at[j])

    def loss_copy(j):
        return pltpu.make_async_copy(loss.at[0, :, columns(j)], inc.at[j], lsem.at[j])

    def out_copy(j):
        return pltpu.make_async_copy(obuf.at[j], out.at[0, 0, :, columns(j)], osem.at[j])

    def filter_copy(slot, peer):
        return pltpu.make_async_remote_copy(
            src_ref=filt, dst_ref=fall.at[slot], send_sem=fsend.at[peer], recv_sem=frecv.at[slot],
            device_id=(stage, peer), device_id_type=MESH_ID,
        )

    def halo_copy(j):
        return pltpu.make_async_remote_copy(
            src_ref=sbuf.at[j], dst_ref=halo.at[j], send_sem=hsend.at[j], recv_sem=hrecv.at[j],
            device_id=(stage, me - 1), device_id_type=MESH_ID,
        )

    def docs_copy():
        return pltpu.make_async_remote_copy(
            src_ref=docs_own, dst_ref=docs_next, send_sem=dsend, recv_sem=drecv,
            device_id=(stage, me - 1), device_id_type=MESH_ID,
        )

    def pipe_copy(j):
        return pltpu.make_async_remote_copy(
            src_ref=obuf.at[j], dst_ref=inc.at[j], send_sem=psend.at[j], recv_sem=precv.at[j],
            device_id=(stage - 1, me), device_id_type=MESH_ID,
        )

    def each(count, fn):
        def step(j, carry):
            fn(j)
            return carry
        lax.fori_loop(0, count, step, 0)

    load_filters = pltpu.make_async_copy(filt_hbm, filt, filt_sem)
    load_docs = pltpu.make_async_copy(docs_hbm, docs, docs_sem)
    load_filters.start()
    load_docs.start()
    each(chunk_count, lambda j: gate_copy(j).start())

    @pl.when(is_last_stage)
    def _():
        each(chunk_count, lambda j: loss_copy(j).start())

    barrier = pltpu.get_barrier_semaphore()

    def greet(k):
        pl.semaphore_signal(
            barrier, inc=1, device_id=(stage, lax.rem(me + k + 1, dp_count)), device_id_type=MESH_ID
        )

    each(dp_count - 1, greet)

    @pl.when(has_below)
    def _():
        pl.semaphore_signal(barrier, inc=1, device_id=(stage - 1, me), device_id_type=MESH_ID)

    @pl.when(not_last_stage)
    def _():
        pl.semaphore_signal(barrier, inc=1, device_id=(stage + 1, me), device_id_type=MESH_ID)

    load_filters.wait()
    load_docs.wait()
    docs_own[...] = jnp.broadcast_to(docs[...], docs_own.shape)
    fall[me] = filt[...]

    greeted = dp_count - 1 + has_below.astype(jnp.int32) + not_last_stage.astype(jnp.int32)
    pl.semaphore_wait(barrier, greeted)

    def send_filters(k):
        peer = lax.rem(me + k + 1, dp_count)
        filter_copy(me, peer).start()

    @pl.when(has_before)
    def _():
        docs_copy().start()

    each(dp_count - 1, send_filters)

    def scale(j):
        gate_copy(j).wait()

        @pl.when(is_last_stage)
        def _():
            loss_copy(j).wait()

        @pl.when(not_last_stage)
        def _():
            pltpu.make_async_remote_copy(
                src_ref=obuf.at[j], dst_ref=inc.at[j], send_sem=psend.at[j], recv_sem=precv.at[j],
                device_id=(stage + 1, me), device_id_type=MESH_ID,
            ).wait_recv()

        sbuf[j] = (gbuf[j].astype(jnp.float32) * inc[j].astype(jnp.float32)).astype(jnp.bfloat16)

        @pl.when(has_before)
        def _():
            halo_copy(j).start()

    @pl.when(is_last_stage)
    def _():
        each(AHEAD, scale)

    @pl.when(jnp.logical_not(has_next))
    def _():
        docs_next[...] = jnp.zeros_like(docs_next)

        def clear(j):
            halo[j] = jnp.zeros((rows, width), jnp.bfloat16)

        each(chunk_count, clear)

    @pl.when(has_next)
    def _():
        pltpu.make_async_remote_copy(
            src_ref=docs_own, dst_ref=docs_next, send_sem=dsend, recv_sem=drecv,
            device_id=(stage, me + 1), device_id_type=MESH_ID,
        ).wait_recv()

    at_row = lax.broadcasted_iota(jnp.int32, (rows, rows), 0)
    at_col = lax.broadcasted_iota(jnp.int32, (rows, rows), 1)
    own_cols = jnp.broadcast_to(docs_own[0:1, :], (rows, rows)).astype(jnp.float32)
    next_cols = jnp.broadcast_to(docs_next[0:1, :], (rows, rows)).astype(jnp.float32)
    own_rows = own_cols.T
    one, zero = jnp.float32(1.0), jnp.float32(0.0)
    mask_own[...] = jnp.where(
        jnp.logical_and(at_col >= at_row, own_rows == own_cols), one, zero
    ).astype(jnp.bfloat16)
    mask_next[...] = jnp.where(
        jnp.logical_and(at_col < at_row, own_rows == next_cols), one, zero
    ).astype(jnp.bfloat16)

    def wait_filters(j):
        for q in range(slots):
            slot = j * slots + q

            @pl.when(slot != me)
            def _():
                filter_copy(slot, slot).wait_recv()


    def produce(j):
        wait_filters(j)

        @pl.when(has_next)
        def _():
            pltpu.make_async_remote_copy(
                src_ref=sbuf.at[j], dst_ref=halo.at[j], send_sem=hsend.at[j], recv_sem=hrecv.at[j],
                device_id=(stage, me + 1), device_id_type=MESH_ID,
            ).wait_recv()

        slab = jnp.concatenate([sbuf[j], halo[j]], axis=0)
        group_of = lax.broadcasted_iota(jnp.int32, (rows, width), 1) // lane_width
        total = inc[j].astype(jnp.float32)
        update = jnp.zeros((rows, width), jnp.float32)
        taps = [fall[j * slots + q].astype(jnp.float32) for q in range(slots)]
        for start in range(0, groups, DOT_GROUPS):
            tables = []
            for g in range(start, start + DOT_GROUPS):
                q, r = divmod(g, slot_groups)
                spread = jnp.broadcast_to(taps[q][r : r + 1, :], (rows, rows))
                turned = pltpu.roll(spread, 0, 1, stride=1, stride_axis=0).astype(jnp.bfloat16)
                tables.append(
                    jnp.concatenate([turned * mask_own[...], turned * mask_next[...]], axis=1)
                )
            parts = jnp.dot(
                jnp.concatenate(tables, axis=0), slab, preferred_element_type=jnp.float32
            )
            for k in range(DOT_GROUPS):
                update = jnp.where(
                    group_of == start + k, parts[k * rows : (k + 1) * rows, :], update
                )
        obuf[j] = (total + update).astype(jnp.bfloat16)

        @pl.when(has_below)
        def _():
            pipe_copy(j).start()

        out_copy(j).start()

    lag = LAG * not_last_stage.astype(jnp.int32)

    def step(s):
        @pl.when(jnp.logical_and(is_last_stage, s + AHEAD < chunk_count))
        def _():
            scale(s + AHEAD)

        @pl.when(jnp.logical_and(not_last_stage, s < chunk_count))
        def _():
            scale(s)

        @pl.when(s >= lag)
        def _():
            produce(s - lag)

    each(chunk_count + lag, step)

    def finish(j):
        out_copy(j).wait()

        @pl.when(has_below)
        def _():
            pipe_copy(j).wait_send()

        @pl.when(has_before)
        def _():
            halo_copy(j).wait_send()

    each(chunk_count, finish)

    @pl.when(has_before)
    def _():
        docs_copy().wait_send()

    each(dp_count - 1, lambda k: filter_copy(me, lax.rem(me + k + 1, dp_count)).wait_send())


def body(mesh_shape, gate, filters, doc_ids, loss_grad):
    dp_count, pipe_count = mesh_shape["dp"], mesh_shape["pipe"]
    _, _, rows, channels = gate.shape
    slot_groups, taps = filters.shape[1:]
    lane_width = channels // (slot_groups * dp_count)
    chunk_count = channels // CHUNK
    slot_rows = -(-slot_groups // 16) * 16
    filt = filters[0]
    if slot_rows != slot_groups:
        filt = jnp.pad(filt, ((0, slot_rows - slot_groups), (0, 0)))
    chunks = pltpu.VMEM((chunk_count, rows, CHUNK), jnp.bfloat16)
    dma = pltpu.SemaphoreType.DMA
    return pl.pallas_call(
        functools.partial(kernel, dp_count, pipe_count, lane_width, slot_groups),
        out_shape=jax.ShapeDtypeStruct(gate.shape, jnp.bfloat16),
        in_specs=[
            pl.BlockSpec(memory_space=pl.ANY),
            pl.BlockSpec(memory_space=pl.ANY),
            pl.BlockSpec(memory_space=pl.ANY),
            pl.BlockSpec(memory_space=pl.ANY),
        ],
        out_specs=pl.BlockSpec(memory_space=pl.ANY),
        scratch_shapes=[
            pltpu.VMEM((slot_rows, taps), jnp.bfloat16),
            pltpu.VMEM((1, rows), jnp.int32),
            dma, dma,
            chunks, chunks, chunks, chunks, chunks,
            pltpu.VMEM((dp_count, slot_rows, taps), jnp.bfloat16),
            pltpu.VMEM((8, rows), jnp.int32),
            pltpu.VMEM((8, rows), jnp.int32),
            pltpu.VMEM((rows, rows), jnp.bfloat16),
            pltpu.VMEM((rows, rows), jnp.bfloat16),
            dma((chunk_count,)), dma((chunk_count,)), dma((chunk_count,)),
            dma((dp_count,)), dma((dp_count,)),
            dma((chunk_count,)), dma((chunk_count,)),
            dma((chunk_count,)), dma((chunk_count,)),
            dma, dma,
        ],
        compiler_params=pltpu.CompilerParams(
            collective_id=0, has_side_effects=True, vmem_limit_bytes=62 * 1024 * 1024
        ),
        cost_estimate=pl.CostEstimate(
            flops=2 * 2 * rows * rows * channels * 16, bytes_accessed=6 * rows * channels, transcendentals=0
        ),
    )(gate, filt, doc_ids, loss_grad)


def solution(mesh):
    return jax.shard_map(
        functools.partial(body, dict(mesh.shape)),
        mesh=mesh,
        in_specs=(
            P("pipe", None, "dp", None),
            P("pipe", "dp", None),
            P(None, "dp"),
            P(None, "dp", None),
        ),
        out_specs=P("pipe", None, "dp", None),
        check_vma=False,
    )
```

```python
import functools

import jax
import jax.numpy as jnp
from jax import lax
from jax.experimental import pallas as pl
from jax.experimental.pallas import tpu as pltpu
from jax.sharding import PartitionSpec as P

MESH_ID = pl.DeviceIdType.MESH
CHUNK = 256
LAG = 2
AHEAD = 3
DOT_GROUPS = 4


def kernel(
    dp_count, pipe_count, lane_width, slot_groups,
    gate, filt_hbm, docs_hbm, loss, out,
    filt, docs, filt_sem, docs_sem, gbuf, inc, sbuf, halo, obuf, fall, docs_own, docs_next, mask_own, mask_next,
    gsem, lsem, osem, fsend, frecv, hsend, hrecv, psend, precv, dsend, drecv,
):
    chunk_count, rows, width = sbuf.shape
    groups = width // lane_width
    slots = groups // slot_groups
    stage = lax.axis_index("pipe")
    me = lax.axis_index("dp")
    is_last_stage = stage == pipe_count - 1
    not_last_stage = stage < pipe_count - 1
    has_below = stage > 0
    has_before = me > 0
    has_next = me < dp_count - 1

    def columns(j):
        return pl.ds(pl.multiple_of(j * width, width), width)

    def gate_copy(j):
        return pltpu.make_async_copy(gate.at[0, 0, :, columns(j)], gbuf.at[j], gsem.at[j])

    def loss_copy(j):
        return pltpu.make_async_copy(loss.at[0, :, columns(j)], inc.at[j], lsem.at[j])

    def out_copy(j):
        return pltpu.make_async_copy(obuf.at[j], out.at[0, 0, :, columns(j)], osem.at[j])

    def filter_copy(slot, peer):
        return pltpu.make_async_remote_copy(
            src_ref=filt, dst_ref=fall.at[slot], send_sem=fsend.at[peer], recv_sem=frecv.at[slot],
            device_id=(stage, peer), device_id_type=MESH_ID,
        )

    def halo_copy(j):
        return pltpu.make_async_remote_copy(
            src_ref=sbuf.at[j], dst_ref=halo.at[j], send_sem=hsend.at[j], recv_sem=hrecv.at[j],
            device_id=(stage, me - 1), device_id_type=MESH_ID,
        )

    def docs_copy():
        return pltpu.make_async_remote_copy(
            src_ref=docs_own, dst_ref=docs_next, send_sem=dsend, recv_sem=drecv,
            device_id=(stage, me - 1), device_id_type=MESH_ID,
        )

    def pipe_copy(j):
        return pltpu.make_async_remote_copy(
            src_ref=obuf.at[j], dst_ref=inc.at[j], send_sem=psend.at[j], recv_sem=precv.at[j],
            device_id=(stage - 1, me), device_id_type=MESH_ID,
        )

    def each(count, fn):
        def step(j, carry):
            fn(j)
            return carry
        lax.fori_loop(0, count, step, 0)

    load_filters = pltpu.make_async_copy(filt_hbm, filt, filt_sem)
    load_docs = pltpu.make_async_copy(docs_hbm, docs, docs_sem)
    load_filters.start()
    load_docs.start()
    each(chunk_count, lambda j: gate_copy(j).start())

    @pl.when(is_last_stage)
    def _():
        each(chunk_count, lambda j: loss_copy(j).start())

    barrier = pltpu.get_barrier_semaphore()

    def greet(k):
        pl.semaphore_signal(
            barrier, inc=1, device_id=(stage, lax.rem(me + k + 1, dp_count)), device_id_type=MESH_ID
        )

    each(dp_count - 1, greet)

    @pl.when(has_below)
    def _():
        pl.semaphore_signal(barrier, inc=1, device_id=(stage - 1, me), device_id_type=MESH_ID)

    @pl.when(not_last_stage)
    def _():
        pl.semaphore_signal(barrier, inc=1, device_id=(stage + 1, me), device_id_type=MESH_ID)

    load_filters.wait()
    load_docs.wait()
    docs_own[...] = jnp.broadcast_to(docs[...], docs_own.shape)
    fall[me] = filt[...]

    greeted = dp_count - 1 + has_below.astype(jnp.int32) + not_last_stage.astype(jnp.int32)
    pl.semaphore_wait(barrier, greeted)

    def send_filters(k):
        peer = lax.rem(me + k + 1, dp_count)
        filter_copy(me, peer).start()

    @pl.when(has_before)
    def _():
        docs_copy().start()

    each(dp_count - 1, send_filters)

    def scale(j):
        gate_copy(j).wait()

        @pl.when(is_last_stage)
        def _():
            loss_copy(j).wait()

        @pl.when(not_last_stage)
        def _():
            pltpu.make_async_remote_copy(
                src_ref=obuf.at[j], dst_ref=inc.at[j], send_sem=psend.at[j], recv_sem=precv.at[j],
                device_id=(stage + 1, me), device_id_type=MESH_ID,
            ).wait_recv()

        sbuf[j] = (gbuf[j].astype(jnp.float32) * inc[j].astype(jnp.float32)).astype(jnp.bfloat16)

        @pl.when(has_before)
        def _():
            halo_copy(j).start()

    @pl.when(is_last_stage)
    def _():
        each(AHEAD, scale)

    @pl.when(jnp.logical_not(has_next))
    def _():
        docs_next[...] = jnp.zeros_like(docs_next)

        def clear(j):
            halo[j] = jnp.zeros((rows, width), jnp.bfloat16)

        each(chunk_count, clear)

    @pl.when(has_next)
    def _():
        pltpu.make_async_remote_copy(
            src_ref=docs_own, dst_ref=docs_next, send_sem=dsend, recv_sem=drecv,
            device_id=(stage, me + 1), device_id_type=MESH_ID,
        ).wait_recv()

    at_row = lax.broadcasted_iota(jnp.int32, (rows, rows), 0)
    at_col = lax.broadcasted_iota(jnp.int32, (rows, rows), 1)
    own_cols = jnp.broadcast_to(docs_own[0:1, :], (rows, rows)).astype(jnp.float32)
    next_cols = jnp.broadcast_to(docs_next[0:1, :], (rows, rows)).astype(jnp.float32)
    own_rows = own_cols.T
    one, zero = jnp.float32(1.0), jnp.float32(0.0)
    mask_own[...] = jnp.where(
        jnp.logical_and(at_col >= at_row, own_rows == own_cols), one, zero
    ).astype(jnp.bfloat16)
    mask_next[...] = jnp.where(
        jnp.logical_and(at_col < at_row, own_rows == next_cols), one, zero
    ).astype(jnp.bfloat16)

    def wait_filters(j):
        for q in range(slots):
            slot = j * slots + q

            @pl.when(slot != me)
            def _():
                filter_copy(slot, slot).wait_recv()


    def produce(j):
        wait_filters(j)

        @pl.when(has_next)
        def _():
            pltpu.make_async_remote_copy(
                src_ref=sbuf.at[j], dst_ref=halo.at[j], send_sem=hsend.at[j], recv_sem=hrecv.at[j],
                device_id=(stage, me + 1), device_id_type=MESH_ID,
            ).wait_recv()

        slab = jnp.concatenate([sbuf[j], halo[j]], axis=0)
        group_of = lax.broadcasted_iota(jnp.int32, (rows, width), 1) // lane_width
        total = inc[j].astype(jnp.float32)
        update = jnp.zeros((rows, width), jnp.float32)
        taps = [fall[j * slots + q].astype(jnp.float32) for q in range(slots)]
        for start in range(0, groups, DOT_GROUPS):
            tables = []
            for g in range(start, start + DOT_GROUPS):
                q, r = divmod(g, slot_groups)
                spread = jnp.broadcast_to(taps[q][r : r + 1, :], (rows, rows))
                turned = pltpu.roll(spread, 0, 1, stride=1, stride_axis=0).astype(jnp.bfloat16)
                tables.append(
                    jnp.concatenate([turned * mask_own[...], turned * mask_next[...]], axis=1)
                )
            parts = jnp.dot(
                jnp.concatenate(tables, axis=0), slab, preferred_element_type=jnp.float32
            )
            for k in range(DOT_GROUPS):
                update = jnp.where(
                    group_of == start + k, parts[k * rows : (k + 1) * rows, :], update
                )
        obuf[j] = (total + update).astype(jnp.bfloat16)

        @pl.when(has_below)
        def _():
            pipe_copy(j).start()

        out_copy(j).start()

    lag = LAG * not_last_stage.astype(jnp.int32)

    def step(s):
        @pl.when(jnp.logical_and(is_last_stage, s + AHEAD < chunk_count))
        def _():
            scale(s + AHEAD)

        @pl.when(jnp.logical_and(not_last_stage, s < chunk_count))
        def _():
            scale(s)

        @pl.when(s >= lag)
        def _():
            produce(s - lag)

    each(chunk_count + lag, step)

    def finish(j):
        out_copy(j).wait()

        @pl.when(has_below)
        def _():
            pipe_copy(j).wait_send()

        @pl.when(has_before)
        def _():
            halo_copy(j).wait_send()

    each(chunk_count, finish)

    @pl.when(has_before)
    def _():
        docs_copy().wait_send()

    each(dp_count - 1, lambda k: filter_copy(me, lax.rem(me + k + 1, dp_count)).wait_send())


def body(mesh_shape, gate, filters, doc_ids, loss_grad):
    dp_count, pipe_count = mesh_shape["dp"], mesh_shape["pipe"]
    _, _, rows, channels = gate.shape
    slot_groups, taps = filters.shape[1:]
    lane_width = channels // (slot_groups * dp_count)
    chunk_count = channels // CHUNK
    slot_rows = -(-slot_groups // 16) * 16
    filt = filters[0]
    if slot_rows != slot_groups:
        filt = jnp.pad(filt, ((0, slot_rows - slot_groups), (0, 0)))
    chunks = pltpu.VMEM((chunk_count, rows, CHUNK), jnp.bfloat16)
    dma = pltpu.SemaphoreType.DMA
    return pl.pallas_call(
        functools.partial(kernel, dp_count, pipe_count, lane_width, slot_groups),
        out_shape=jax.ShapeDtypeStruct(gate.shape, jnp.bfloat16),
        in_specs=[
            pl.BlockSpec(memory_space=pl.ANY),
            pl.BlockSpec(memory_space=pl.ANY),
            pl.BlockSpec(memory_space=pl.ANY),
            pl.BlockSpec(memory_space=pl.ANY),
        ],
        out_specs=pl.BlockSpec(memory_space=pl.ANY),
        scratch_shapes=[
            pltpu.VMEM((slot_rows, taps), jnp.bfloat16),
            pltpu.VMEM((1, rows), jnp.int32),
            dma, dma,
            chunks, chunks, chunks, chunks, chunks,
            pltpu.VMEM((dp_count, slot_rows, taps), jnp.bfloat16),
            pltpu.VMEM((8, rows), jnp.int32),
            pltpu.VMEM((8, rows), jnp.int32),
            pltpu.VMEM((rows, rows), jnp.bfloat16),
            pltpu.VMEM((rows, rows), jnp.bfloat16),
            dma((chunk_count,)), dma((chunk_count,)), dma((chunk_count,)),
            dma((dp_count,)), dma((dp_count,)),
            dma((chunk_count,)), dma((chunk_count,)),
            dma((chunk_count,)), dma((chunk_count,)),
            dma, dma,
        ],
        compiler_params=pltpu.CompilerParams(
            collective_id=0, has_side_effects=True, vmem_limit_bytes=62 * 1024 * 1024
        ),
        cost_estimate=pl.CostEstimate(
            flops=2 * 2 * rows * rows * channels * 16, bytes_accessed=6 * rows * channels, transcendentals=0
        ),
    )(gate, filt, doc_ids, loss_grad)


def solution(mesh):
    return jax.shard_map(
        functools.partial(body, dict(mesh.shape)),
        mesh=mesh,
        in_specs=(
            P("pipe", None, "dp", None),
            P("pipe", "dp", None),
            P(None, "dp"),
            P(None, "dp", None),
        ),
        out_specs=P("pipe", None, "dp", None),
        check_vma=False,
    )
```
